512 devices in a mesh: group: 16 (over x_hi, y), blk: 32 (over z, x_lo, core).
Axes of the slice: x: 4 (x_hi: 2, x_lo: 2; x = x_hi * 2 + x_lo), y: 8, z: 8, core: 2. Of those that a mesh axis runs over, the one named last changes fastest.
Arguments:
- queries: bfloat16 [32768, 2560], P(('group', 'blk')), may hold values from -6 to 6
- keys: bfloat16 [32768, 2560], P(('group', 'blk')), may hold values from -6 to 6
- values: bfloat16 [32768, 2560], P(('group', 'blk')), may hold values from -6 to 6
- stale_keys: bfloat16 [32768, 2560], P(('group', 'blk')), may hold values from -6 to 6
- stale_values: bfloat16 [32768, 2560], P(('group', 'blk')), may hold values from -6 to 6
- patch_order: int32 [32768], P(('group', 'blk')), may hold values from 0 to 63, as said below
- stale_age: int32 [16], replicated, may hold values from 0 to 3
Outputs:
- attended: bfloat16 [32768, 2560], P(('group', 'blk'))
The draws below stay inside these ranges and needn't reach their ends.
Inputs may be any that keep to these rules, and one draw needn't show every extreme that they name: `patch_order`: each device's block of 64 entries is a permutation of 0 .. 63.
All inputs are finite; a program needn't handle non-finite values.
Results may differ from the reference program's by a relative error of at most 0.0046.
Values may be sent and summed in bfloat16 or wider, within the bound.
A program may use at most 64 MiB of HBM per device.

```python
import jax
import jax.numpy as jnp
from jax import lax

HEAD_DIM = 128
HEADS = 20
TOK_DEV = 64
POOL = 4
REACH = 3
TOKENS = 32768
GROUPS = 16
N_GROUP = 16
N_BLK = 32


def draw_queries(key, part):
    key = jax.random.fold_in(key, 11)
    result = jnp.clip(jax.random.normal(key, (TOKENS, HEADS * HEAD_DIM), jnp.float32), -6.0, 6.0)
    return result.astype(jnp.bfloat16)


def draw_keys(key, part):
    key = jax.random.fold_in(key, 23)
    result = jnp.clip(jax.random.normal(key, (TOKENS, HEADS * HEAD_DIM), jnp.float32), -6.0, 6.0)
    return result.astype(jnp.bfloat16)


def draw_patch_order(key, part):
    key = jax.random.fold_in(key, 37)
    blocks = TOKENS // TOK_DEV
    block_keys = jax.random.split(key, blocks)
    perms = jax.vmap(lambda k: jax.random.permutation(k, TOK_DEV))(block_keys)
    return perms.reshape(TOKENS).astype(jnp.int32)


def with_ends(values, stream_key, smallest, top_value):
    place = [jax.random.randint(jax.random.fold_in(stream_key, axis), (), 0, length) for axis, length in enumerate(values.shape)]
    longest = values.shape.index(max(values.shape))
    beside = place[:longest] + [(place[longest] + 1) % values.shape[longest]] + place[longest + 1:]
    return values.at[tuple(place)].set(smallest).at[tuple(beside)].set(top_value)


def steps_of(own_key, dims, shards, low, top_value):
    def one(position, parts):
        steps = jax.random.uniform(jax.random.fold_in(jax.random.fold_in(own_key, 6), position), (parts,), jnp.float32, low / len(shards), top_value / len(shards))
        return jnp.repeat(jnp.exp(steps), dims[position] // parts).reshape((-1,) + (1,) * (len(dims) - position - 1))

    level = one(*shards[0])
    for cut in shards[1:]:
        level = level * one(*cut)
    return level


def scatter_about(key, dims, scale, limit, cuts=(), held_as=jnp.bfloat16):
    gain = steps_of(key, dims, cuts, -0.22, 0.18) if cuts else 1.0
    entries = jax.random.normal(key, dims, jnp.float32) * scale * gain
    return jnp.minimum(jnp.maximum(entries, -limit), limit).astype(held_as)


def setup_inputs(seed: int = 0) -> dict:
    arg_keys = jax.random.split(jax.random.key(seed), 8)
    return {
        "queries": draw_queries(jax.random.fold_in(arg_keys[7], 71), 0),
        "keys": draw_keys(jax.random.fold_in(arg_keys[7], 71), 0),
        "values": scatter_about(arg_keys[2], (TOKENS, HEADS * HEAD_DIM), 1.0, 6.0, ((0, 512),)),
        "stale_keys": scatter_about(arg_keys[3], (TOKENS, HEADS * HEAD_DIM), 1.0, 6.0, ((0, 512),)),
        "stale_values": scatter_about(arg_keys[4], (TOKENS, HEADS * HEAD_DIM), 1.0, 6.0, ((0, 512),)),
        "patch_order": draw_patch_order(jax.random.fold_in(arg_keys[7], 71), 0),
        "stale_age": with_ends(jax.random.randint(arg_keys[6], (GROUPS,), 0, 4), jax.random.fold_in(arg_keys[6], 1), 0, 3).astype(jnp.int32),
    }


age_penalty = 0.5
masked = -1e+30

def attend(query, fresh_k, fresh_v, pool_k, pool_v, bias):
    heads = HEADS
    rows = query.shape[0]
    all_k = jnp.concatenate([fresh_k, pool_k], axis=0)
    all_v = jnp.concatenate([fresh_v, pool_v], axis=0)
    count = all_k.shape[0]
    qh = query.reshape(rows, heads, HEAD_DIM).astype(jnp.float32)
    kh = all_k.reshape(count, heads, HEAD_DIM).astype(jnp.float32)
    vh = all_v.reshape(count, heads, HEAD_DIM).astype(jnp.float32)
    scores = jnp.einsum('qhd,khd->hqk', qh, kh) / jnp.sqrt(jnp.float32(HEAD_DIM)) + bias[None, None, :]
    peak = lax.optimization_barrier(jnp.max(scores, axis=-1, keepdims=True))
    expo = jnp.exp(scores - peak)
    total = lax.optimization_barrier(jnp.sum(expo, axis=-1))
    weights = expo.astype(jnp.bfloat16).astype(jnp.float32)
    summed = jnp.einsum('hqk,khd->qhd', weights, vh)
    return (summed / jnp.transpose(total)[:, :, None]).reshape(rows, heads * HEAD_DIM).astype(jnp.bfloat16)

def reference(queries, keys, values, stale_keys, stale_values, patch_order, stale_age):
    rows = TOK_DEV
    groups = N_GROUP
    tiles = N_BLK
    width = HEADS * HEAD_DIM
    pooled_rows = rows // POOL
    order = patch_order.reshape(groups * tiles, rows).astype(jnp.int32)

    def pool(stale):
        blocks = stale.reshape(groups * tiles, rows, width)

        def one(pair):
            block, idx = pair
            picked = jnp.take(block, idx, axis=0).astype(jnp.float32)
            return lax.optimization_barrier(jnp.mean(picked.reshape(pooled_rows, POOL, width), axis=1)).astype(jnp.bfloat16)
        pooled = lax.map(one, (blocks, order))
        return jnp.transpose(pooled.reshape(groups, tiles, pooled_rows, width), (1, 0, 2, 3)).reshape(tiles, groups * pooled_rows, width)
    pool_k = pool(stale_keys)
    pool_v = pool(stale_values)
    qg = queries.reshape(groups, tiles, rows, width)
    kg = keys.reshape(groups, tiles, rows, width)
    vg = values.reshape(groups, tiles, rows, width)
    penalty = -age_penalty * stale_age.astype(jnp.float32)

    def per_group(index):
        g = index.astype(jnp.int32)
        q_here = lax.dynamic_index_in_dim(qg, g, 0, keepdims=False)
        k_here = lax.dynamic_index_in_dim(kg, g, 0, keepdims=False)
        v_here = lax.dynamic_index_in_dim(vg, g, 0, keepdims=False)
        fresh_k = jnp.concatenate([jnp.roll(k_here, -d, axis=0) for d in range(-REACH, REACH + 1)], axis=1)
        fresh_v = jnp.concatenate([jnp.roll(v_here, -d, axis=0) for d in range(-REACH, REACH + 1)], axis=1)
        group_bias = jnp.where(jnp.arange(groups, dtype=jnp.int32) == g, jnp.float32(masked), penalty)
        bias = jnp.concatenate([jnp.zeros(((2 * REACH + 1) * rows,), jnp.float32), jnp.repeat(group_bias, pooled_rows)])

        def per_tile(pack):
            return attend(pack[0], pack[1], pack[2], pack[3], pack[4], bias)
        return lax.map(per_tile, (q_here, fresh_k, fresh_v, pool_k, pool_v))
    result = lax.map(per_group, jnp.arange(groups, dtype=jnp.int32))
    return result.reshape(groups * tiles * rows, width)
```

```python
import functools

import jax
import jax.numpy as jnp
from jax import lax
from jax.experimental import pallas as pl
from jax.experimental.pallas import tpu as pltpu
from jax.sharding import PartitionSpec as P

MESH = pl.DeviceIdType.MESH
HEAD_DIM = 128
POOL = 4
LOG2E = 1.4426950408889634
AGE_PENALTY = 0.5
MASKED = -1e30
UNROLL = 5

OWN, OTHER, X, XF, ZD, ZF, ZFF = 0, 64, 128, 192, 256, 384, 448
POOLED = {
    ("own", 0, 0): 320,
    ("par", 0, 0): 336,
    ("own", 1, 1): 352,
    ("own", 1, -1): 368,
    ("par", 1, 1): 512,
    ("par", 1, -1): 528,
    ("own", 2, 1): 544,
    ("own", 2, -1): 560,
    ("par", 2, 1): 576,
    ("par", 2, -1): 592,
    ("own", 3, 1): 608,
    ("own", 3, -1): 624,
    ("par", 3, 1): 640,
    ("par", 3, -1): 656,
    ("own", 4, 1): 672,
    ("par", 4, 1): 688,
}
ROWS = 704


def copy_ids():
    ids = {}
    for kv in (0, 1):
        for name in ("other", "x", "zd", "xf", "zf", "zff"):
            ids[(name, kv)] = len(ids)
        ids[("par0", kv)] = len(ids)
        for col in ("own", "par"):
            for dist in (1, 2, 3):
                for way in (1, -1):
                    ids[(col, dist, way, kv)] = len(ids)
            ids[(col, 4, 1, kv)] = len(ids)
    return ids


IDS = copy_ids()


def kernel(
    q_hbm, k_hbm, v_hbm, sk_hbm, sv_hbm, order_ref, age_ref, out_ref,
    kbuf, vbuf, q, sk, sv, acc, top, part, ssem, rsem, lsem,
):
    g, b = lax.axis_index("group"), lax.axis_index("blk")
    xh, y = g // 8, g % 8
    z, xl, c = b // 4, (b // 2) % 2, b % 2

    def at(xh_, y_, z_, xl_, c_):
        return (xh_ * 8 + y_, z_ * 4 + xl_ * 2 + c_)

    other = at(xh, y, z, xl, 1 - c)
    xpeer = at(xh, y, z, 1 - xl, c)
    zup, zdown = at(xh, y, (z + 1) % 8, xl, c), at(xh, y, (z + 7) % 8, xl, c)
    zdirect = at(xh, y, (z + 7 + 2 * c) % 8, xl, 1 - c)
    zforward = at(xh, y, (z + 1 + 6 * xl) % 8, xl, c)
    ynext = {1: at(xh, (y + 1) % 8, z, xl, c), -1: at(xh, (y + 7) % 8, z, xl, c)}
    partner = at(1 - xh, y, z, xl, c)

    barrier = pltpu.get_barrier_semaphore()
    everyone = (other, xpeer, zup, zdown, zdirect, ynext[1], ynext[-1], partner)
    for device in everyone:
        pl.semaphore_signal(barrier, inc=1, device_id=device, device_id_type=MESH)

    bufs = (kbuf, vbuf)
    fresh = (k_hbm, v_hbm)
    loads = [
        pltpu.make_async_copy(src, dst, lsem.at[i])
        for i, (src, dst) in enumerate(
            (
                (sk_hbm, sk),
                (sv_hbm, sv),
                (q_hbm, q),
                (k_hbm, kbuf.at[pl.ds(OWN, 64)]),
                (v_hbm, vbuf.at[pl.ds(OWN, 64)]),
            )
        )
    ]
    for load in loads:
        load.start()

    def rows(kv, slot, count):
        return bufs[kv].at[pl.ds(slot, count)]

    def remote(key, src, dst, device):
        i = IDS[key]
        return pltpu.make_async_remote_copy(
            src_ref=src, dst_ref=dst, send_sem=ssem.at[i], recv_sem=rsem.at[i],
            device_id=device, device_id_type=MESH,
        )

    sent = []

    def send(key, src, dst, device):
        copy = remote(key, src, dst, device)
        copy.start()
        sent.append(copy)

    def arrived(key, dst):
        remote(key, dst, dst, other).wait_recv()

    t = lax.broadcasted_iota(jnp.int32, (64, 64), 0)
    picks = jnp.where(t == order_ref[...], 1.0, 0.0).astype(jnp.bfloat16)
    j = lax.broadcasted_iota(jnp.int32, (16, 64), 0)
    r = lax.broadcasted_iota(jnp.int32, (16, 64), 1)
    quarter = jnp.where(r // POOL == j, 1.0 / POOL, 0.0).astype(jnp.bfloat16)
    average = lax.dot_general(
        quarter, picks, (((1,), (1,)), ((), ())), preferred_element_type=jnp.float32
    ).astype(jnp.bfloat16)
    mine = POOLED[("own", 0, 0)]
    for kv, stale in enumerate((sk, sv)):
        loads[kv].wait()
        bufs[kv][pl.ds(mine, 16), :] = jnp.dot(
            average, stale[...], preferred_element_type=jnp.float32
        ).astype(jnp.bfloat16)

    pl.semaphore_wait(barrier, len(everyone))

    for kv in (0, 1):
        block = rows(kv, mine, 16)
        for way in (1, -1):
            send(("own", 1, way, kv), block, rows(kv, POOLED[("own", 1, way)], 16), ynext[way])
        send(("par0", kv), block, rows(kv, POOLED[("par", 0, 0)], 16), partner)
    for kv in (0, 1):
        send(("other", kv), fresh[kv], rows(kv, OTHER, 64), other)
        send(("x", kv), fresh[kv], rows(kv, X, 64), xpeer)
        send(("zd", kv), fresh[kv], rows(kv, ZD, 64), zdirect)

    def pass_on(col, dist, way, kv):
        slot = POOLED[(col, dist, way)]
        if dist:
            arrived((col, dist, way, kv), rows(kv, slot, 16))
        if dist < 3:
            send((col, dist + 1, way, kv), rows(kv, slot, 16), rows(kv, POOLED[(col, dist + 1, way)], 16), ynext[way])
        elif kv == (0 if way == 1 else 1):
            send((col, 4, 1, kv), rows(kv, slot, 16), rows(kv, POOLED[(col, 4, 1)], 16), ynext[way])

    def ring(col, dist):
        for kv in (0, 1):
            for way in (1, -1):
                pass_on(col, dist, way, kv)

    lane = lax.broadcasted_iota(jnp.int32, (1, 128), 1)

    def penalty(slot):
        col, dist, way = slot
        if slot == ("own", 0, 0):
            return jnp.float32(MASKED * LOG2E)
        half = xh if col == "own" else 1 - xh
        group = half * 8 + (y + 8 - way * dist) % 8
        return age_ref[group].astype(jnp.float32) * jnp.float32(-AGE_PENALTY * LOG2E)

    def bias_of(start, count):
        found = [(o - start, s) for s, o in POOLED.items() if start <= o < start + count]
        if not found:
            return None
        bias = jnp.zeros((1, count), jnp.float32)
        for offset, slot in found:
            here = (lane[:, :count] >= offset) & (lane[:, :count] < offset + 16)
            bias = jnp.where(here, penalty(slot), bias)
        return bias

    scale = LOG2E / (HEAD_DIM ** 0.5)
    heads = q.shape[1] // HEAD_DIM

    def attend(start, count, first=False, last=False):
        bias = bias_of(start, count)

        def head(h):
            cols = pl.ds(pl.multiple_of(h * HEAD_DIM, HEAD_DIM), HEAD_DIM)
            s = lax.dot_general(
                q[:, cols], kbuf[pl.ds(start, count), cols], (((1,), (1,)), ((), ())),
                preferred_element_type=jnp.float32,
            ) * scale
            if bias is not None:
                s = s + bias
            peak = jnp.max(s, axis=-1, keepdims=True)
            if first:
                old, new = None, jnp.broadcast_to(peak, (64, HEAD_DIM))
            else:
                old = top[:, cols]
                new = jnp.maximum(old, peak)
            p = jnp.exp2(s - new[:, :count])
            add = jnp.dot(
                p.astype(jnp.bfloat16), vbuf[pl.ds(start, count), cols],
                preferred_element_type=jnp.float32,
            )
            if count < HEAD_DIM:
                p = jnp.concatenate([p, jnp.zeros((64, HEAD_DIM - count), jnp.float32)], axis=1)
            if first:
                total, value = p, add
            else:
                keep = jnp.exp2(old - new)
                total = part[:, cols] * keep + p
                value = acc[:, cols] * keep + add
            if last:
                total = jnp.sum(total, axis=-1, keepdims=True)
                out_ref[:, cols] = (value / total).astype(jnp.bfloat16)
            else:
                top[:, cols] = new
                part[:, cols] = total
                acc[:, cols] = value

        @pl.loop(0, heads // UNROLL)
        def _(step):
            for u in range(UNROLL):
                head(step * UNROLL + u)

    for load in loads[2:]:
        load.wait()
    for kv in (0, 1):
        arrived(("other", kv), rows(kv, OTHER, 64))
    attend(OWN, 128, first=True)
    for kv in (0, 1):
        arrived(("par0", kv), rows(kv, POOLED[("par", 0, 0)], 16))
        block = rows(kv, POOLED[("par", 0, 0)], 16)
        for way in (1, -1):
            send(("par", 1, way, kv), block, rows(kv, POOLED[("par", 1, way)], 16), ynext[way])
    ring("own", 1)
    for kv in (0, 1):
        tile = rows(kv, X, 64)
        arrived(("x", kv), tile)
        send(("zf", kv), tile, rows(kv, ZF, 64), zforward)
        send(("xf", kv), tile, rows(kv, XF, 64), other)
    for kv in (0, 1):
        arrived(("zd", kv), rows(kv, ZD, 64))
    attend(ZD, 128)
    ring("par", 1)
    ring("own", 2)
    for kv in (0, 1):
        arrived(("xf", kv), rows(kv, XF, 64))
    attend(X, 128)
    ring("par", 2)
    for kv in (0, 1):
        tile = rows(kv, ZF, 64)
        arrived(("zf", kv), tile)
        send(("zff", kv), tile, rows(kv, ZFF, 64), other)
    for kv in (0, 1):
        arrived(("zff", kv), rows(kv, ZFF, 64))
    attend(ZF, 128)
    ring("own", 3)
    attend(POOLED[("par", 1, 1)], 128)
    ring("par", 3)
    for kv in (0, 1):
        for col in ("own", "par"):
            arrived((col, 4, 1, kv), rows(kv, POOLED[(col, 4, 1)], 16))
    attend(POOLED[("par", 3, 1)], 64, last=True)
    for copy in sent:
        copy.wait_send()


def body(queries, keys, values, stale_keys, stale_values, patch_order, stale_age):
    rows, width = queries.shape
    copies = len(IDS)
    wide = (rows, width)
    return pl.pallas_call(
        kernel,
        out_shape=jax.ShapeDtypeStruct(wide, jnp.bfloat16),
        in_specs=[pl.BlockSpec(memory_space=pl.ANY)] * 5
        + [pl.BlockSpec(memory_space=pltpu.VMEM), pl.BlockSpec(memory_space=pltpu.SMEM)],
        out_specs=pl.BlockSpec(memory_space=pltpu.VMEM),
        scratch_shapes=[
            pltpu.VMEM((ROWS, width), jnp.bfloat16),
            pltpu.VMEM((ROWS, width), jnp.bfloat16),
            pltpu.VMEM(wide, jnp.bfloat16),
            pltpu.VMEM(wide, jnp.bfloat16),
            pltpu.VMEM(wide, jnp.bfloat16),
            pltpu.VMEM(wide, jnp.float32),
            pltpu.VMEM(wide, jnp.float32),
            pltpu.VMEM(wide, jnp.float32),
            pltpu.SemaphoreType.DMA((copies,)),
            pltpu.SemaphoreType.DMA((copies,)),
            pltpu.SemaphoreType.DMA((5,)),
        ],
        name="tile_attention",
        compiler_params=pltpu.CompilerParams(
            collective_id=0, has_side_effects=True, vmem_limit_bytes=56 * 1024 * 1024
        ),
    )(queries, keys, values, stale_keys, stale_values, patch_order.reshape(1, rows), stale_age)


def solution(mesh):
    tokens = P(("group", "blk"), None)
    return jax.shard_map(
        body,
        mesh=mesh,
        in_specs=(tokens, tokens, tokens, tokens, tokens, P(("group", "blk")), P()),
        out_specs=tokens,
        check_vma=False,
    )
```

```python
import functools

import jax
import jax.numpy as jnp
from jax import lax
from jax.experimental import pallas as pl
from jax.experimental.pallas import tpu as pltpu
from jax.sharding import PartitionSpec as P

MESH = pl.DeviceIdType.MESH
HEAD_DIM = 128
POOL = 4
LOG2E = 1.4426950408889634
AGE_PENALTY = 0.5
MASKED = -1e30
UNROLL = 20
PARTS = 2

OWN, OTHER, X, XF, ZD, ZF, ZFF = 0, 64, 128, 192, 256, 384, 448
POOLED = {
    ("own", 0, 0): 320,
    ("par", 0, 0): 336,
    ("own", 1, 1): 352,
    ("own", 1, -1): 368,
    ("own", 2, 1): 512,
    ("own", 2, -1): 528,
    ("own", 3, 1): 544,
    ("own", 3, -1): 560,
    ("own", 4, 1): 576,
    ("par", 1, 1): 592,
    ("par", 1, -1): 608,
    ("par", 2, 1): 624,
    ("par", 2, -1): 640,
    ("par", 3, 1): 656,
    ("par", 3, -1): 672,
    ("par", 4, 1): 688,
}
ROWS = 704


def copy_ids():
    ids = {}
    for kv in (0, 1):
        for name in ("other", "x", "zd", "xf", "zf", "zff"):
            for part in range(PARTS):
                ids[(name, kv, part)] = len(ids)
        ids[("par0", kv)] = len(ids)
        for col in ("own", "par"):
            for dist in (1, 2, 3):
                for way in (1, -1):
                    ids[(col, dist, way, kv)] = len(ids)
            ids[(col, 4, 1, kv)] = len(ids)
    return ids


IDS = copy_ids()


def kernel(
    q_hbm, k_hbm, v_hbm, sk_hbm, sv_hbm, order_ref, age_ref, out_ref,
    kbuf, vbuf, q, sk, sv, acc, top, part, ssem, rsem, lsem, zsem,
):
    g, b = lax.axis_index("group"), lax.axis_index("blk")
    xh, y = g // 8, g % 8
    z, xl, c = b // 4, (b // 2) % 2, b % 2

    def at(xh_, y_, z_, xl_, c_):
        return (xh_ * 8 + y_, z_ * 4 + xl_ * 2 + c_)

    other = at(xh, y, z, xl, 1 - c)
    xpeer = at(xh, y, z, 1 - xl, c)
    zup, zdown = at(xh, y, (z + 1) % 8, xl, c), at(xh, y, (z + 7) % 8, xl, c)
    zdirect = at(xh, y, (z + 7 + 2 * c) % 8, xl, 1 - c)
    zforward = at(xh, y, (z + 1 + 6 * xl) % 8, xl, c)
    ynext = {1: at(xh, (y + 1) % 8, z, xl, c), -1: at(xh, (y + 7) % 8, z, xl, c)}
    partner = at(1 - xh, y, z, xl, c)

    barrier = pltpu.get_barrier_semaphore()
    plane = (other, xpeer, ynext[1], ynext[-1], partner)
    across = (zup, zdown, zdirect)
    odd = z % 2

    def signal(semaphore, devices):
        for device in devices:
            pl.semaphore_signal(semaphore, inc=1, device_id=device, device_id_type=MESH)

    signal(barrier, plane)

    @pl.when(odd == 0)
    def _():
        signal(barrier, across)

    bufs = (kbuf, vbuf)
    fresh = (k_hbm, v_hbm)
    loads = [
        pltpu.make_async_copy(src, dst, lsem.at[i])
        for i, (src, dst) in enumerate(
            (
                (sk_hbm, sk),
                (sv_hbm, sv),
                (q_hbm, q),
                (k_hbm, kbuf.at[pl.ds(OWN, 64)]),
                (v_hbm, vbuf.at[pl.ds(OWN, 64)]),
            )
        )
    ]
    for load in loads:
        load.start()

    def rows(kv, slot, count):
        return bufs[kv].at[pl.ds(slot, count)]

    def remote(key, src, dst, device):
        i = IDS[key]
        return pltpu.make_async_remote_copy(
            src_ref=src, dst_ref=dst, send_sem=ssem.at[i], recv_sem=rsem.at[i],
            device_id=device, device_id_type=MESH,
        )

    sent = []

    def send(key, src, dst, device):
        copy = remote(key, src, dst, device)
        copy.start()
        sent.append(copy)

    def arrived(key, dst):
        remote(key, dst, dst, other).wait_recv()

    t = lax.broadcasted_iota(jnp.int32, (64, 64), 0)
    picks = jnp.where(t == order_ref[...], 1.0, 0.0).astype(jnp.bfloat16)
    j = lax.broadcasted_iota(jnp.int32, (16, 64), 0)
    r = lax.broadcasted_iota(jnp.int32, (16, 64), 1)
    quarter = jnp.where(r // POOL == j, 1.0 / POOL, 0.0).astype(jnp.bfloat16)
    average = lax.dot_general(
        quarter, picks, (((1,), (1,)), ((), ())), preferred_element_type=jnp.float32
    ).astype(jnp.bfloat16)
    mine = POOLED[("own", 0, 0)]
    for kv, stale in enumerate((sk, sv)):
        loads[kv].wait()
        bufs[kv][pl.ds(mine, 16), :] = jnp.dot(
            average, stale[...], preferred_element_type=jnp.float32
        ).astype(jnp.bfloat16)

    pl.semaphore_wait(barrier, len(plane) + len(across) * odd)

    @pl.when(odd == 1)
    def _():
        signal(zsem, across)

    for kv in (0, 1):
        block = rows(kv, mine, 16)
        for way in (1, -1):
            send(("own", 1, way, kv), block, rows(kv, POOLED[("own", 1, way)], 16), ynext[way])
        send(("par0", kv), block, rows(kv, POOLED[("par", 0, 0)], 16), partner)
    span = q.shape[1] // PARTS

    def piece(ref, part):
        return ref.at[:, pl.ds(part * span, span)]

    def tile(kv, slot, part):
        return piece(rows(kv, slot, 64), part)

    every = [(kv, part) for kv in (0, 1) for part in range(PARTS)]
    for kv, n in every:
        source = piece(fresh[kv], n)
        send(("x", kv, n), source, tile(kv, X, n), xpeer)
        send(("other", kv, n), source, tile(kv, OTHER, n), other)

    def open_z():
        @pl.when(odd == 0)
        def _():
            pl.semaphore_wait(zsem, len(across))

        for kv, n in every:
            remote(("zd", kv, n), piece(fresh[kv], n), tile(kv, ZD, n), zdirect).start()

    pl.when(z != 0)(open_z)

    def landed(name, slot):
        for kv, n in every:
            arrived((name, kv, n), tile(kv, slot, n))

    def pass_x(kv, part):
        here = tile(kv, X, part)
        arrived(("x", kv, part), here)
        send(("zf", kv, part), here, tile(kv, ZF, part), zforward)
        send(("xf", kv, part), here, tile(kv, XF, part), other)

    def pass_z(kv, part):
        here = tile(kv, ZF, part)
        arrived(("zf", kv, part), here)
        send(("zff", kv, part), here, tile(kv, ZFF, part), other)

    def pass_on(col, dist, way, kv):
        here = rows(kv, POOLED[(col, dist, way)], 16)
        arrived((col, dist, way, kv), here)
        if dist < 3:
            send((col, dist + 1, way, kv), here, rows(kv, POOLED[(col, dist + 1, way)], 16), ynext[way])
        elif col == "own" and kv == (0 if way == 1 else 1):
            send((col, 4, 1, kv), here, rows(kv, POOLED[(col, 4, 1)], 16), ynext[way])

    def pass_far(kv):
        here = rows(kv, POOLED[("own", 4, 1)], 16)
        arrived(("own", 4, 1, kv), here)
        send(("par", 4, 1, kv), here, rows(kv, POOLED[("par", 4, 1)], 16), partner)

    def ring(col, dist, kvs=(0, 1)):
        for kv in kvs:
            for way in (1, -1):
                pass_on(col, dist, way, kv)

    lane = lax.broadcasted_iota(jnp.int32, (1, 128), 1)

    def penalty(slot):
        col, dist, way = slot
        if slot == ("own", 0, 0):
            return jnp.float32(MASKED * LOG2E)
        half = xh if col == "own" else 1 - xh
        group = half * 8 + (y + 8 - way * dist) % 8
        return age_ref[group].astype(jnp.float32) * jnp.float32(-AGE_PENALTY * LOG2E)

    def bias_of(start, count):
        found = [(o - start, s) for s, o in POOLED.items() if start <= o < start + count]
        if not found:
            return None
        bias = jnp.zeros((1, count), jnp.float32)
        for offset, slot in found:
            here = (lane[:, :count] >= offset) & (lane[:, :count] < offset + 16)
            bias = jnp.where(here, penalty(slot), bias)
        return bias

    scale = LOG2E / (HEAD_DIM ** 0.5)
    heads = q.shape[1] // HEAD_DIM

    def attend(start, count, first=False, last=False):
        bias = bias_of(start, count)

        def block(first_head):
            cols = [
                pl.ds(pl.multiple_of((first_head + u) * HEAD_DIM, HEAD_DIM), HEAD_DIM)
                for u in range(UNROLL)
            ]
            scores = [
                lax.dot_general(
                    q[:, c], kbuf[pl.ds(start, count), c], (((1,), (1,)), ((), ())),
                    preferred_element_type=jnp.float32,
                )
                for c in cols
            ]
            scores = [s * scale if bias is None else s * scale + bias for s in scores]
            peaks = [jnp.max(s, axis=-1, keepdims=True) for s in scores]
            if first:
                tops = [jnp.broadcast_to(peak, (64, HEAD_DIM)) for peak in peaks]
            else:
                olds = [top[:, c] for c in cols]
                tops = [jnp.maximum(old, peak) for old, peak in zip(olds, peaks)]
                keeps = [jnp.exp2(old - new) for old, new in zip(olds, tops)]
            weights = [jnp.exp2(s - new[:, :count]) for s, new in zip(scores, tops)]
            values = [
                jnp.dot(
                    p.astype(jnp.bfloat16), vbuf[pl.ds(start, count), c],
                    preferred_element_type=jnp.float32,
                )
                for p, c in zip(weights, cols)
            ]
            if count < HEAD_DIM:
                rest = jnp.zeros((64, HEAD_DIM - count), jnp.float32)
                weights = [jnp.concatenate([p, rest], axis=1) for p in weights]
            if not first:
                weights = [part[:, c] * keep + p for c, keep, p in zip(cols, keeps, weights)]
                values = [acc[:, c] * keep + v for c, keep, v in zip(cols, keeps, values)]
            if last:
                totals = [jnp.sum(p, axis=-1, keepdims=True) for p in weights]
                for c, total, value in zip(cols, totals, values):
                    out_ref[:, c] = (value / total).astype(jnp.bfloat16)
            else:
                for c, new, p, value in zip(cols, tops, weights, values):
                    top[:, c] = new
                    part[:, c] = p
                    acc[:, c] = value

        @pl.loop(0, heads // UNROLL)
        def _(step):
            block(step * UNROLL)

    for load in loads[2:]:
        load.wait()
    landed("other", OTHER)
    attend(OWN, 128, first=True)
    ring("own", 1)
    pl.when(z == 0)(open_z)
    sent.extend(
        remote(("zd", kv, n), piece(fresh[kv], n), tile(kv, ZD, n), zdirect) for kv, n in every
    )
    pass_x(0, 0)
    ring("own", 2)
    for kv in (0, 1):
        block = rows(kv, POOLED[("par", 0, 0)], 16)
        arrived(("par0", kv), block)
        for way in (1, -1):
            send(("par", 1, way, kv), block, rows(kv, POOLED[("par", 1, way)], 16), ynext[way])
    pass_x(0, 1)
    landed("zd", ZD)
    attend(ZD, 128)
    ring("own", 3)
    pass_x(1, 0)
    ring("par", 1)
    pass_z(0, 0)
    pass_far(0)
    pass_far(1)
    pass_x(1, 1)
    pass_z(0, 1)
    landed("xf", XF)
    attend(X, 128)
    ring("par", 2)
    pass_z(1, 0)
    attend(POOLED[("own", 2, 1)], 128)
    pass_z(1, 1)
    landed("zff", ZFF)
    attend(ZF, 128)
    ring("par", 3)
    for kv in (0, 1):
        arrived(("par", 4, 1, kv), rows(kv, POOLED[("par", 4, 1)], 16))
    attend(POOLED[("par", 2, -1)], 64, last=True)
    for copy in sent:
        copy.wait_send()


def body(queries, keys, values, stale_keys, stale_values, patch_order, stale_age):
    rows, width = queries.shape
    copies = len(IDS)
    wide = (rows, width)
    return pl.pallas_call(
        kernel,
        out_shape=jax.ShapeDtypeStruct(wide, jnp.bfloat16),
        in_specs=[pl.BlockSpec(memory_space=pl.ANY)] * 5
        + [pl.BlockSpec(memory_space=pltpu.VMEM), pl.BlockSpec(memory_space=pltpu.SMEM)],
        out_specs=pl.BlockSpec(memory_space=pltpu.VMEM),
        scratch_shapes=[
            pltpu.VMEM((ROWS, width), jnp.bfloat16),
            pltpu.VMEM((ROWS, width), jnp.bfloat16),
            pltpu.VMEM(wide, jnp.bfloat16),
            pltpu.VMEM(wide, jnp.bfloat16),
            pltpu.VMEM(wide, jnp.bfloat16),
            pltpu.VMEM(wide, jnp.float32),
            pltpu.VMEM(wide, jnp.float32),
            pltpu.VMEM(wide, jnp.float32),
            pltpu.SemaphoreType.DMA((copies,)),
            pltpu.SemaphoreType.DMA((copies,)),
            pltpu.SemaphoreType.DMA((5,)),
            pltpu.SemaphoreType.REGULAR,
        ],
        name="tile_attention",
        compiler_params=pltpu.CompilerParams(
            collective_id=0, has_side_effects=True, vmem_limit_bytes=56 * 1024 * 1024
        ),
    )(queries, keys, values, stale_keys, stale_values, patch_order.reshape(1, rows), stale_age)


def solution(mesh):
    tokens = P(("group", "blk"), None)
    return jax.shard_map(
        body,
        mesh=mesh,
        in_specs=(tokens, tokens, tokens, tokens, tokens, P(("group", "blk")), P()),
        out_specs=tokens,
        check_vma=False,
    )
```

```python
import functools

import jax
import jax.numpy as jnp
from jax import lax
from jax.experimental import pallas as pl
from jax.experimental.pallas import tpu as pltpu
from jax.sharding import PartitionSpec as P

MESH = pl.DeviceIdType.MESH
HEAD_DIM = 128
POOL = 4
LOG2E = 1.4426950408889634
AGE_PENALTY = 0.5
MASKED = -1e30
UNROLL = 20
PARTS = 2

OWN, OTHER, X, XF, ZD, ZF, ZFF = 0, 64, 128, 192, 256, 384, 448
POOLED = {
    ("own", 0, 0): 320,
    ("par", 0, 0): 336,
    ("own", 1, 1): 352,
    ("own", 1, -1): 368,
    ("own", 2, 1): 512,
    ("own", 2, -1): 528,
    ("own", 3, 1): 544,
    ("own", 3, -1): 560,
    ("own", 4, 1): 576,
    ("par", 1, 1): 592,
    ("par", 1, -1): 608,
    ("par", 2, 1): 624,
    ("par", 2, -1): 640,
    ("par", 3, 1): 656,
    ("par", 3, -1): 672,
    ("par", 4, 1): 688,
}
ROWS = 704


def copy_ids():
    ids = {}
    for kv in (0, 1):
        for name in ("other", "x", "zd", "xf", "zf", "zff"):
            for part in range(PARTS):
                ids[(name, kv, part)] = len(ids)
        ids[("par0", kv)] = len(ids)
        for col in ("own", "par"):
            for dist in (1, 2, 3):
                for way in (1, -1):
                    ids[(col, dist, way, kv)] = len(ids)
            ids[(col, 4, 1, kv)] = len(ids)
    return ids


IDS = copy_ids()


def kernel(
    q_hbm, k_hbm, v_hbm, sk_hbm, sv_hbm, order_ref, age_ref, out_ref,
    kbuf, vbuf, q, sk, sv, acc, top, part, ssem, rsem, lsem, zsem,
):
    g, b = lax.axis_index("group"), lax.axis_index("blk")
    xh, y = g // 8, g % 8
    z, xl, c = b // 4, (b // 2) % 2, b % 2

    def at(xh_, y_, z_, xl_, c_):
        return (xh_ * 8 + y_, z_ * 4 + xl_ * 2 + c_)

    other = at(xh, y, z, xl, 1 - c)
    xpeer = at(xh, y, z, 1 - xl, c)
    zup, zdown = at(xh, y, (z + 1) % 8, xl, c), at(xh, y, (z + 7) % 8, xl, c)
    zdirect = at(xh, y, (z + 7 + 2 * c) % 8, xl, 1 - c)
    zforward = at(xh, y, (z + 1 + 6 * xl) % 8, xl, c)
    ynext = {1: at(xh, (y + 1) % 8, z, xl, c), -1: at(xh, (y + 7) % 8, z, xl, c)}
    partner = at(1 - xh, y, z, xl, c)

    barrier = pltpu.get_barrier_semaphore()
    plane = (other, xpeer, ynext[1], ynext[-1], partner)
    across = (zup, zdown, zdirect)
    odd = z % 2

    def signal(semaphore, devices):
        for device in devices:
            pl.semaphore_signal(semaphore, inc=1, device_id=device, device_id_type=MESH)

    signal(barrier, plane)

    @pl.when(odd == 0)
    def _():
        signal(barrier, across)

    bufs = (kbuf, vbuf)
    fresh = (k_hbm, v_hbm)
    loads = [
        pltpu.make_async_copy(src, dst, lsem.at[i])
        for i, (src, dst) in enumerate(
            (
                (sk_hbm, sk),
                (sv_hbm, sv),
                (q_hbm, q),
                (k_hbm, kbuf.at[pl.ds(OWN, 64)]),
                (v_hbm, vbuf.at[pl.ds(OWN, 64)]),
            )
        )
    ]
    for load in loads[:2]:
        load.start()

    def rows(kv, slot, count):
        return bufs[kv].at[pl.ds(slot, count)]

    def remote(key, src, dst, device):
        i = IDS[key]
        return pltpu.make_async_remote_copy(
            src_ref=src, dst_ref=dst, send_sem=ssem.at[i], recv_sem=rsem.at[i],
            device_id=device, device_id_type=MESH,
        )

    sent = []

    def send(key, src, dst, device):
        copy = remote(key, src, dst, device)
        copy.start()
        sent.append(copy)

    def arrived(key, dst):
        remote(key, dst, dst, other).wait_recv()

    t = lax.broadcasted_iota(jnp.int32, (64, 64), 0)
    picks = jnp.where(t == order_ref[...], 1.0, 0.0).astype(jnp.bfloat16)
    j = lax.broadcasted_iota(jnp.int32, (16, 64), 0)
    r = lax.broadcasted_iota(jnp.int32, (16, 64), 1)
    quarter = jnp.where(r // POOL == j, 1.0 / POOL, 0.0).astype(jnp.bfloat16)
    average = lax.dot_general(
        quarter, picks, (((1,), (1,)), ((), ())), preferred_element_type=jnp.float32
    ).astype(jnp.bfloat16)
    mine = POOLED[("own", 0, 0)]

    def pool(kv):
        loads[kv].wait()
        bufs[kv][pl.ds(mine, 16), :] = jnp.dot(
            average, (sk, sv)[kv][...], preferred_element_type=jnp.float32
        ).astype(jnp.bfloat16)

    def send_pooled(kv):
        block = rows(kv, mine, 16)
        for way in (1, -1):
            send(("own", 1, way, kv), block, rows(kv, POOLED[("own", 1, way)], 16), ynext[way])
        send(("par0", kv), block, rows(kv, POOLED[("par", 0, 0)], 16), partner)

    pool(0)
    pl.semaphore_wait(barrier, len(plane) + len(across) * odd)

    @pl.when(odd == 1)
    def _():
        signal(zsem, across)

    send_pooled(0)
    pool(1)
    send_pooled(1)
    for load in loads[2:]:
        load.start()

    span = q.shape[1] // PARTS

    def piece(ref, part):
        return ref.at[:, pl.ds(part * span, span)]

    def tile(kv, slot, part):
        return piece(rows(kv, slot, 64), part)

    every = [(kv, part) for kv in (0, 1) for part in range(PARTS)]
    for kv, n in every:
        source = piece(fresh[kv], n)
        send(("x", kv, n), source, tile(kv, X, n), xpeer)
        send(("other", kv, n), source, tile(kv, OTHER, n), other)

    def open_z():
        @pl.when(odd == 0)
        def _():
            pl.semaphore_wait(zsem, len(across))

        for kv, n in every:
            remote(("zd", kv, n), piece(fresh[kv], n), tile(kv, ZD, n), zdirect).start()

    pl.when(z != 0)(open_z)

    def landed(name, slot):
        for kv, n in every:
            arrived((name, kv, n), tile(kv, slot, n))

    def pass_x(kv, part):
        here = tile(kv, X, part)
        arrived(("x", kv, part), here)
        send(("zf", kv, part), here, tile(kv, ZF, part), zforward)
        send(("xf", kv, part), here, tile(kv, XF, part), other)

    def pass_z(kv, part):
        here = tile(kv, ZF, part)
        arrived(("zf", kv, part), here)
        send(("zff", kv, part), here, tile(kv, ZFF, part), other)

    def pass_on(col, dist, way, kv):
        here = rows(kv, POOLED[(col, dist, way)], 16)
        arrived((col, dist, way, kv), here)
        if dist < 3:
            send((col, dist + 1, way, kv), here, rows(kv, POOLED[(col, dist + 1, way)], 16), ynext[way])
        elif col == "own" and kv == (0 if way == 1 else 1):
            send((col, 4, 1, kv), here, rows(kv, POOLED[(col, 4, 1)], 16), ynext[way])

    def pass_far(kv):
        here = rows(kv, POOLED[("own", 4, 1)], 16)
        arrived(("own", 4, 1, kv), here)
        send(("par", 4, 1, kv), here, rows(kv, POOLED[("par", 4, 1)], 16), partner)

    def ring(col, dist, kvs=(0, 1)):
        for kv in kvs:
            for way in (1, -1):
                pass_on(col, dist, way, kv)

    lane = lax.broadcasted_iota(jnp.int32, (1, 128), 1)

    def penalty(slot):
        col, dist, way = slot
        if slot == ("own", 0, 0):
            return jnp.float32(MASKED * LOG2E)
        half = xh if col == "own" else 1 - xh
        group = half * 8 + (y + 8 - way * dist) % 8
        return age_ref[group].astype(jnp.float32) * jnp.float32(-AGE_PENALTY * LOG2E)

    def bias_of(start, count):
        found = [(o - start, s) for s, o in POOLED.items() if start <= o < start + count]
        if not found:
            return None
        bias = jnp.zeros((1, count), jnp.float32)
        for offset, slot in found:
            here = (lane[:, :count] >= offset) & (lane[:, :count] < offset + 16)
            bias = jnp.where(here, penalty(slot), bias)
        return bias

    scale = LOG2E / (HEAD_DIM ** 0.5)
    heads = q.shape[1] // HEAD_DIM

    def attend(start, count, first=False, last=False):
        bias = bias_of(start, count)

        def block(first_head):
            cols = [
                pl.ds(pl.multiple_of((first_head + u) * HEAD_DIM, HEAD_DIM), HEAD_DIM)
                for u in range(UNROLL)
            ]
            scores = [
                lax.dot_general(
                    q[:, c], kbuf[pl.ds(start, count), c], (((1,), (1,)), ((), ())),
                    preferred_element_type=jnp.float32,
                )
                for c in cols
            ]
            scores = [s * scale if bias is None else s * scale + bias for s in scores]
            peaks = [jnp.max(s, axis=-1, keepdims=True) for s in scores]
            if first:
                tops = [jnp.broadcast_to(peak, (64, HEAD_DIM)) for peak in peaks]
            else:
                olds = [top[:, c] for c in cols]
                tops = [jnp.maximum(old, peak) for old, peak in zip(olds, peaks)]
                keeps = [jnp.exp2(old - new) for old, new in zip(olds, tops)]
            weights = [jnp.exp2(s - new[:, :count]) for s, new in zip(scores, tops)]
            values = [
                jnp.dot(
                    p.astype(jnp.bfloat16), vbuf[pl.ds(start, count), c],
                    preferred_element_type=jnp.float32,
                )
                for p, c in zip(weights, cols)
            ]
            if count < HEAD_DIM:
                rest = jnp.zeros((64, HEAD_DIM - count), jnp.float32)
                weights = [jnp.concatenate([p, rest], axis=1) for p in weights]
            if not first:
                weights = [part[:, c] * keep + p for c, keep, p in zip(cols, keeps, weights)]
                values = [acc[:, c] * keep + v for c, keep, v in zip(cols, keeps, values)]
            if last:
                totals = [jnp.sum(p, axis=-1, keepdims=True) for p in weights]
                for c, total, value in zip(cols, totals, values):
                    out_ref[:, c] = (value / total).astype(jnp.bfloat16)
            else:
                for c, new, p, value in zip(cols, tops, weights, values):
                    top[:, c] = new
                    part[:, c] = p
                    acc[:, c] = value

        @pl.loop(0, heads // UNROLL)
        def _(step):
            block(step * UNROLL)

    for load in loads[2:]:
        load.wait()
    landed("other", OTHER)
    attend(OWN, 128, first=True)
    ring("own", 1)
    pl.when(z == 0)(open_z)
    sent.extend(
        remote(("zd", kv, n), piece(fresh[kv], n), tile(kv, ZD, n), zdirect) for kv, n in every
    )
    pass_x(0, 0)
    ring("own", 2)
    for kv in (0, 1):
        block = rows(kv, POOLED[("par", 0, 0)], 16)
        arrived(("par0", kv), block)
        for way in (1, -1):
            send(("par", 1, way, kv), block, rows(kv, POOLED[("par", 1, way)], 16), ynext[way])
    pass_x(0, 1)
    landed("zd", ZD)
    attend(ZD, 128)
    ring("own", 3)
    pass_x(1, 0)
    ring("par", 1)
    pass_z(0, 0)
    pass_far(0)
    pass_far(1)
    pass_x(1, 1)
    pass_z(0, 1)
    landed("xf", XF)
    attend(X, 128)
    ring("par", 2)
    pass_z(1, 0)
    attend(POOLED[("own", 2, 1)], 128)
    pass_z(1, 1)
    landed("zff", ZFF)
    attend(ZF, 128)
    ring("par", 3)
    for kv in (0, 1):
        arrived(("par", 4, 1, kv), rows(kv, POOLED[("par", 4, 1)], 16))
    attend(POOLED[("par", 2, -1)], 64, last=True)
    for copy in sent:
        copy.wait_send()


def body(queries, keys, values, stale_keys, stale_values, patch_order, stale_age):
    rows, width = queries.shape
    copies = len(IDS)
    wide = (rows, width)
    return pl.pallas_call(
        kernel,
        out_shape=pltpu.VMEM(wide, jnp.bfloat16),
        in_specs=[pl.BlockSpec(memory_space=pl.ANY)] * 5
        + [pl.BlockSpec(memory_space=pltpu.VMEM), pl.BlockSpec(memory_space=pltpu.SMEM)],
        out_specs=pl.BlockSpec(memory_space=pltpu.VMEM),
        scratch_shapes=[
            pltpu.VMEM((ROWS, width), jnp.bfloat16),
            pltpu.VMEM((ROWS, width), jnp.bfloat16),
            pltpu.VMEM(wide, jnp.bfloat16),
            pltpu.VMEM(wide, jnp.bfloat16),
            pltpu.VMEM(wide, jnp.bfloat16),
            pltpu.VMEM(wide, jnp.float32),
            pltpu.VMEM(wide, jnp.float32),
            pltpu.VMEM(wide, jnp.float32),
            pltpu.SemaphoreType.DMA((copies,)),
            pltpu.SemaphoreType.DMA((copies,)),
            pltpu.SemaphoreType.DMA((5,)),
            pltpu.SemaphoreType.REGULAR,
        ],
        name="tile_attention",
        compiler_params=pltpu.CompilerParams(
            collective_id=0, has_side_effects=True, vmem_limit_bytes=56 * 1024 * 1024
        ),
    )(queries, keys, values, stale_keys, stale_values, patch_order.reshape(1, rows), stale_age)


def solution(mesh):
    tokens = P(("group", "blk"), None)
    return jax.shard_map(
        body,
        mesh=mesh,
        in_specs=(tokens, tokens, tokens, tokens, tokens, P(("group", "blk")), P()),
        out_specs=tokens,
        check_vma=False,
    )
```

```python
import functools

import jax
import jax.numpy as jnp
from jax import lax
from jax.experimental import pallas as pl
from jax.experimental.pallas import tpu as pltpu
from jax.sharding import PartitionSpec as P

MESH = pl.DeviceIdType.MESH
HEAD_DIM = 128
POOL = 4
LOG2E = 1.4426950408889634
AGE_PENALTY = 0.5
MASKED = -1e30
UNROLL = 20
PARTS = 2

OWN, OTHER, X, XF, ZD, ZF, ZFF = 0, 64, 128, 192, 256, 384, 448
POOLED = {
    ("own", 0, 0): 320,
    ("par", 0, 0): 336,
    ("own", 1, 1): 352,
    ("own", 1, -1): 368,
    ("own", 2, 1): 512,
    ("own", 2, -1): 528,
    ("own", 3, 1): 544,
    ("own", 3, -1): 560,
    ("own", 4, 1): 576,
    ("par", 1, 1): 592,
    ("par", 1, -1): 608,
    ("par", 2, 1): 624,
    ("par", 2, -1): 640,
    ("par", 3, 1): 656,
    ("par", 3, -1): 672,
    ("par", 4, 1): 688,
}
ROWS = 704


def copy_ids():
    ids = {}
    for kv in (0, 1):
        for name in ("other", "x", "zd", "xf", "zf", "zff"):
            for part in range(PARTS):
                ids[(name, kv, part)] = len(ids)
        ids[("par0", kv)] = len(ids)
        for col in ("own", "par"):
            for dist in (1, 2, 3):
                for way in (1, -1):
                    ids[(col, dist, way, kv)] = len(ids)
            ids[(col, 4, 1, kv)] = len(ids)
    return ids


IDS = copy_ids()


def kernel(
    q_hbm, k_hbm, v_hbm, sk_hbm, sv_hbm, order_ref, age_ref, out_ref,
    kbuf, vbuf, q, sk, sv, acc, top, part, ssem, rsem, lsem, zsem,
):
    g, b = lax.axis_index("group"), lax.axis_index("blk")
    xh, y = g // 8, g % 8
    z, xl, c = b // 4, (b // 2) % 2, b % 2

    def at(xh_, y_, z_, xl_, c_):
        return (xh_ * 8 + y_, z_ * 4 + xl_ * 2 + c_)

    other = at(xh, y, z, xl, 1 - c)
    xpeer = at(xh, y, z, 1 - xl, c)
    zup, zdown = at(xh, y, (z + 1) % 8, xl, c), at(xh, y, (z + 7) % 8, xl, c)
    zdirect = at(xh, y, (z + 7 + 2 * c) % 8, xl, 1 - c)
    zforward = at(xh, y, (z + 1 + 6 * xl) % 8, xl, c)
    ynext = {1: at(xh, (y + 1) % 8, z, xl, c), -1: at(xh, (y + 7) % 8, z, xl, c)}
    partner = at(1 - xh, y, z, xl, c)

    bufs = (kbuf, vbuf)
    fresh = (k_hbm, v_hbm)
    loads = [
        pltpu.make_async_copy(src, dst, lsem.at[i])
        for i, (src, dst) in enumerate(
            (
                (sk_hbm, sk),
                (sv_hbm, sv),
                (q_hbm, q),
                (k_hbm, kbuf.at[pl.ds(OWN, 64)]),
                (v_hbm, vbuf.at[pl.ds(OWN, 64)]),
            )
        )
    ]
    for load in loads[:2]:
        load.start()

    barrier = pltpu.get_barrier_semaphore()
    plane = (other, xpeer, ynext[1], ynext[-1], partner)
    across = (zup, zdown, zdirect)
    odd = z % 2

    def signal(semaphore, devices):
        for device in devices:
            pl.semaphore_signal(semaphore, inc=1, device_id=device, device_id_type=MESH)

    signal(barrier, plane)

    @pl.when(odd == 0)
    def _():
        signal(barrier, across)

    def rows(kv, slot, count):
        return bufs[kv].at[pl.ds(slot, count)]

    def remote(key, src, dst, device):
        i = IDS[key]
        return pltpu.make_async_remote_copy(
            src_ref=src, dst_ref=dst, send_sem=ssem.at[i], recv_sem=rsem.at[i],
            device_id=device, device_id_type=MESH,
        )

    sent = []

    def send(key, src, dst, device):
        copy = remote(key, src, dst, device)
        copy.start()
        sent.append(copy)

    def arrived(key, dst):
        remote(key, dst, dst, other).wait_recv()

    t = lax.broadcasted_iota(jnp.int32, (64, 64), 0)
    picks = jnp.where(t == order_ref[...], 1.0, 0.0).astype(jnp.bfloat16)
    j = lax.broadcasted_iota(jnp.int32, (16, 64), 0)
    r = lax.broadcasted_iota(jnp.int32, (16, 64), 1)
    quarter = jnp.where(r // POOL == j, 1.0 / POOL, 0.0).astype(jnp.bfloat16)
    average = lax.dot_general(
        quarter, picks, (((1,), (1,)), ((), ())), preferred_element_type=jnp.float32
    ).astype(jnp.bfloat16)
    mine = POOLED[("own", 0, 0)]

    def pool(kv):
        loads[kv].wait()
        bufs[kv][pl.ds(mine, 16), :] = jnp.dot(
            average, (sk, sv)[kv][...], preferred_element_type=jnp.float32
        ).astype(jnp.bfloat16)

    def send_pooled(kv):
        block = rows(kv, mine, 16)
        for way in (1, -1):
            send(("own", 1, way, kv), block, rows(kv, POOLED[("own", 1, way)], 16), ynext[way])
        send(("par0", kv), block, rows(kv, POOLED[("par", 0, 0)], 16), partner)

    pool(0)
    pl.semaphore_wait(barrier, len(plane) + len(across) * odd)

    @pl.when(odd == 1)
    def _():
        signal(zsem, across)

    send_pooled(0)
    pool(1)
    send_pooled(1)
    for load in loads[2:]:
        load.start()

    span = q.shape[1] // PARTS

    def piece(ref, part):
        return ref.at[:, pl.ds(part * span, span)]

    def tile(kv, slot, part):
        return piece(rows(kv, slot, 64), part)

    every = [(kv, part) for kv in (0, 1) for part in range(PARTS)]
    for kv, n in every:
        source = piece(fresh[kv], n)
        send(("x", kv, n), source, tile(kv, X, n), xpeer)
        send(("other", kv, n), source, tile(kv, OTHER, n), other)

    def open_z():
        @pl.when(odd == 0)
        def _():
            pl.semaphore_wait(zsem, len(across))

        for kv, n in every:
            remote(("zd", kv, n), piece(fresh[kv], n), tile(kv, ZD, n), zdirect).start()

    pl.when(z != 0)(open_z)

    def landed(name, slot):
        for kv, n in every:
            arrived((name, kv, n), tile(kv, slot, n))

    def pass_x(kv, part):
        here = tile(kv, X, part)
        arrived(("x", kv, part), here)
        send(("zf", kv, part), here, tile(kv, ZF, part), zforward)
        send(("xf", kv, part), here, tile(kv, XF, part), other)

    def pass_z(kv, part):
        here = tile(kv, ZF, part)
        arrived(("zf", kv, part), here)
        send(("zff", kv, part), here, tile(kv, ZFF, part), other)

    def pass_on(col, dist, way, kv):
        here = rows(kv, POOLED[(col, dist, way)], 16)
        arrived((col, dist, way, kv), here)
        if dist < 3:
            send((col, dist + 1, way, kv), here, rows(kv, POOLED[(col, dist + 1, way)], 16), ynext[way])
        elif col == "own" and kv == (0 if way == 1 else 1):
            send((col, 4, 1, kv), here, rows(kv, POOLED[(col, 4, 1)], 16), ynext[way])

    def pass_far(kv):
        here = rows(kv, POOLED[("own", 4, 1)], 16)
        arrived(("own", 4, 1, kv), here)
        send(("par", 4, 1, kv), here, rows(kv, POOLED[("par", 4, 1)], 16), partner)

    def ring(col, dist, kvs=(0, 1)):
        for kv in kvs:
            for way in (1, -1):
                pass_on(col, dist, way, kv)

    lane = lax.broadcasted_iota(jnp.int32, (1, 128), 1)

    def penalty(slot):
        col, dist, way = slot
        if slot == ("own", 0, 0):
            return jnp.float32(MASKED * LOG2E)
        half = xh if col == "own" else 1 - xh
        group = half * 8 + (y + 8 - way * dist) % 8
        return age_ref[group].astype(jnp.float32) * jnp.float32(-AGE_PENALTY * LOG2E)

    def bias_of(start, count):
        found = [(o - start, s) for s, o in POOLED.items() if start <= o < start + count]
        if not found:
            return None
        bias = jnp.zeros((1, count), jnp.float32)
        for offset, slot in found:
            here = (lane[:, :count] >= offset) & (lane[:, :count] < offset + 16)
            bias = jnp.where(here, penalty(slot), bias)
        return bias

    scale = LOG2E / (HEAD_DIM ** 0.5)
    heads = q.shape[1] // HEAD_DIM

    def attend(start, count, first=False, last=False):
        bias = bias_of(start, count)

        def block(first_head):
            cols = [
                pl.ds(pl.multiple_of((first_head + u) * HEAD_DIM, HEAD_DIM), HEAD_DIM)
                for u in range(UNROLL)
            ]
            scores = [
                lax.dot_general(
                    q[:, c], kbuf[pl.ds(start, count), c], (((1,), (1,)), ((), ())),
                    preferred_element_type=jnp.float32,
                )
                for c in cols
            ]
            scores = [s * scale if bias is None else s * scale + bias for s in scores]
            peaks = [jnp.max(s, axis=-1, keepdims=True) for s in scores]
            if first:
                tops = [jnp.broadcast_to(peak, (64, HEAD_DIM)) for peak in peaks]
            else:
                olds = [top[:, c] for c in cols]
                tops = [jnp.maximum(old, peak) for old, peak in zip(olds, peaks)]
                keeps = [jnp.exp2(old - new) for old, new in zip(olds, tops)]
            weights = [jnp.exp2(s - new[:, :count]) for s, new in zip(scores, tops)]
            values = [
                jnp.dot(
                    p.astype(jnp.bfloat16), vbuf[pl.ds(start, count), c],
                    preferred_element_type=jnp.float32,
                )
                for p, c in zip(weights, cols)
            ]
            if count < HEAD_DIM:
                rest = jnp.zeros((64, HEAD_DIM - count), jnp.float32)
                weights = [jnp.concatenate([p, rest], axis=1) for p in weights]
            if not first:
                weights = [part[:, c] * keep + p for c, keep, p in zip(cols, keeps, weights)]
                values = [acc[:, c] * keep + v for c, keep, v in zip(cols, keeps, values)]
            if last:
                totals = [jnp.sum(p, axis=-1, keepdims=True) for p in weights]
                for c, total, value in zip(cols, totals, values):
                    out_ref[:, c] = (value / total).astype(jnp.bfloat16)
            else:
                for c, new, p, value in zip(cols, tops, weights, values):
                    top[:, c] = new
                    part[:, c] = p
                    acc[:, c] = value

        @pl.loop(0, heads // UNROLL)
        def _(step):
            block(step * UNROLL)

    for load in loads[2:]:
        load.wait()
    landed("other", OTHER)
    attend(OWN, 128, first=True)
    ring("own", 1)
    pl.when(z == 0)(open_z)
    sent.extend(
        remote(("zd", kv, n), piece(fresh[kv], n), tile(kv, ZD, n), zdirect) for kv, n in every
    )
    pass_x(0, 0)
    ring("own", 2)
    for kv in (0, 1):
        block = rows(kv, POOLED[("par", 0, 0)], 16)
        arrived(("par0", kv), block)
        for way in (1, -1):
            send(("par", 1, way, kv), block, rows(kv, POOLED[("par", 1, way)], 16), ynext[way])
    pass_x(0, 1)
    landed("zd", ZD)
    attend(ZD, 128)
    ring("own", 3)
    pass_x(1, 0)
    ring("par", 1)
    pass_z(0, 0)
    pass_far(0)
    pass_far(1)
    pass_x(1, 1)
    pass_z(0, 1)
    landed("xf", XF)
    attend(X, 128)
    ring("par", 2)
    pass_z(1, 0)
    attend(POOLED[("own", 2, 1)], 128)
    pass_z(1, 1)
    ring("par", 3)
    for kv in (0, 1):
        arrived(("par", 4, 1, kv), rows(kv, POOLED[("par", 4, 1)], 16))
    attend(POOLED[("par", 2, -1)], 64)
    landed("zff", ZFF)
    attend(ZF, 128, last=True)
    for copy in sent:
        copy.wait_send()


def body(queries, keys, values, stale_keys, stale_values, patch_order, stale_age):
    rows, width = queries.shape
    copies = len(IDS)
    wide = (rows, width)
    return pl.pallas_call(
        kernel,
        out_shape=pltpu.VMEM(wide, jnp.bfloat16),
        in_specs=[pl.BlockSpec(memory_space=pl.ANY)] * 5
        + [pl.BlockSpec(memory_space=pltpu.VMEM), pl.BlockSpec(memory_space=pltpu.SMEM)],
        out_specs=pl.BlockSpec(memory_space=pltpu.VMEM),
        scratch_shapes=[
            pltpu.VMEM((ROWS, width), jnp.bfloat16),
            pltpu.VMEM((ROWS, width), jnp.bfloat16),
            pltpu.VMEM(wide, jnp.bfloat16),
            pltpu.VMEM(wide, jnp.bfloat16),
            pltpu.VMEM(wide, jnp.bfloat16),
            pltpu.VMEM(wide, jnp.float32),
            pltpu.VMEM(wide, jnp.float32),
            pltpu.VMEM(wide, jnp.float32),
            pltpu.SemaphoreType.DMA((copies,)),
            pltpu.SemaphoreType.DMA((copies,)),
            pltpu.SemaphoreType.DMA((5,)),
            pltpu.SemaphoreType.REGULAR,
        ],
        name="tile_attention",
        compiler_params=pltpu.CompilerParams(
            collective_id=0, has_side_effects=True, vmem_limit_bytes=56 * 1024 * 1024
        ),
    )(queries, keys, values, stale_keys, stale_values, patch_order.reshape(1, rows), stale_age)


def solution(mesh):
    tokens = P(("group", "blk"), None)
    return jax.shard_map(
        body,
        mesh=mesh,
        in_specs=(tokens, tokens, tokens, tokens, tokens, P(("group", "blk")), P()),
        out_specs=tokens,
        check_vma=False,
    )
```

```python
import functools

import jax
import jax.numpy as jnp
from jax import lax
from jax.experimental import pallas as pl
from jax.experimental.pallas import tpu as pltpu
from jax.sharding import PartitionSpec as P

MESH = pl.DeviceIdType.MESH
HEAD_DIM = 128
POOL = 4
LOG2E = 1.4426950408889634
AGE_PENALTY = 0.5
MASKED = -1e30
UNROLL = 20
PARTS = 2

OWN, OTHER, X, XF, ZD, ZF, ZFF = 0, 64, 128, 192, 256, 384, 448
POOLED = {
    ("own", 0, 0): 320,
    ("par", 0, 0): 336,
    ("own", 1, 1): 352,
    ("own", 1, -1): 368,
    ("own", 2, 1): 512,
    ("own", 2, -1): 528,
    ("own", 3, 1): 544,
    ("own", 3, -1): 560,
    ("own", 4, 1): 576,
    ("par", 1, 1): 592,
    ("par", 1, -1): 608,
    ("par", 2, 1): 624,
    ("par", 2, -1): 640,
    ("par", 3, 1): 656,
    ("par", 3, -1): 672,
    ("par", 4, 1): 688,
}
ROWS = 704


def copy_ids():
    ids = {}
    for kv in (0, 1):
        for name in ("other", "x", "zd", "xf", "zf", "zff"):
            for part in range(PARTS):
                ids[(name, kv, part)] = len(ids)
        ids[("par0", kv)] = len(ids)
        for col in ("own", "par"):
            for dist in (1, 2, 3):
                for way in (1, -1):
                    ids[(col, dist, way, kv)] = len(ids)
            ids[(col, 4, 1, kv)] = len(ids)
    return ids


IDS = copy_ids()


def kernel(
    q_hbm, k_hbm, v_hbm, sk_hbm, sv_hbm, order_ref, age_ref, out_ref,
    kbuf, vbuf, q, sk, sv, acc, top, part, ssem, rsem, lsem, zsem,
):
    g, b = lax.axis_index("group"), lax.axis_index("blk")
    xh, y = g // 8, g % 8
    z, xl, c = b // 4, (b // 2) % 2, b % 2

    def at(xh_, y_, z_, xl_, c_):
        return (xh_ * 8 + y_, z_ * 4 + xl_ * 2 + c_)

    other = at(xh, y, z, xl, 1 - c)
    xpeer = at(xh, y, z, 1 - xl, c)
    zup, zdown = at(xh, y, (z + 1) % 8, xl, c), at(xh, y, (z + 7) % 8, xl, c)
    zdirect = at(xh, y, (z + 7 + 2 * c) % 8, xl, 1 - c)
    zforward = at(xh, y, (z + 1 + 6 * xl) % 8, xl, c)
    ynext = {1: at(xh, (y + 1) % 8, z, xl, c), -1: at(xh, (y + 7) % 8, z, xl, c)}
    partner = at(1 - xh, y, z, xl, c)

    bufs = (kbuf, vbuf)
    fresh = (k_hbm, v_hbm)
    loads = [
        pltpu.make_async_copy(src, dst, lsem.at[i])
        for i, (src, dst) in enumerate(
            (
                (sk_hbm, sk),
                (sv_hbm, sv),
                (q_hbm, q),
                (k_hbm, kbuf.at[pl.ds(OWN, 64)]),
                (v_hbm, vbuf.at[pl.ds(OWN, 64)]),
            )
        )
    ]
    for load in loads[:2]:
        load.start()

    barrier = pltpu.get_barrier_semaphore()
    plane = (other, xpeer, ynext[1], ynext[-1], partner)
    across = (zup, zdown, zdirect)
    odd = z % 2

    def signal(semaphore, devices):
        for device in devices:
            pl.semaphore_signal(semaphore, inc=1, device_id=device, device_id_type=MESH)

    signal(barrier, plane)

    @pl.when(odd == 0)
    def _():
        signal(barrier, across)

    def rows(kv, slot, count):
        return bufs[kv].at[pl.ds(slot, count)]

    def remote(key, src, dst, device):
        i = IDS[key]
        return pltpu.make_async_remote_copy(
            src_ref=src, dst_ref=dst, send_sem=ssem.at[i], recv_sem=rsem.at[i],
            device_id=device, device_id_type=MESH,
        )

    sent = []

    def send(key, src, dst, device):
        copy = remote(key, src, dst, device)
        copy.start()
        sent.append(copy)

    def arrived(key, dst):
        remote(key, dst, dst, other).wait_recv()

    t = lax.broadcasted_iota(jnp.int32, (64, 64), 0)
    picks = jnp.where(t == order_ref[...], 1.0, 0.0).astype(jnp.bfloat16)
    j = lax.broadcasted_iota(jnp.int32, (16, 64), 0)
    r = lax.broadcasted_iota(jnp.int32, (16, 64), 1)
    quarter = jnp.where(r // POOL == j, 1.0 / POOL, 0.0).astype(jnp.bfloat16)
    average = lax.dot_general(
        quarter, picks, (((1,), (1,)), ((), ())), preferred_element_type=jnp.float32
    ).astype(jnp.bfloat16)
    mine = POOLED[("own", 0, 0)]

    def pool(kv):
        loads[kv].wait()
        bufs[kv][pl.ds(mine, 16), :] = jnp.dot(
            average, (sk, sv)[kv][...], preferred_element_type=jnp.float32
        ).astype(jnp.bfloat16)

    def send_pooled(kv):
        block = rows(kv, mine, 16)
        for way in (1, -1):
            send(("own", 1, way, kv), block, rows(kv, POOLED[("own", 1, way)], 16), ynext[way])
        send(("par0", kv), block, rows(kv, POOLED[("par", 0, 0)], 16), partner)

    pool(0)
    pl.semaphore_wait(barrier, len(plane) + len(across) * odd)

    @pl.when(odd == 1)
    def _():
        signal(zsem, across)

    send_pooled(0)
    pool(1)
    send_pooled(1)
    for load in loads[2:]:
        load.start()

    span = q.shape[1] // PARTS

    def piece(ref, part):
        return ref.at[:, pl.ds(part * span, span)]

    def tile(kv, slot, part):
        return piece(rows(kv, slot, 64), part)

    every = [(kv, part) for kv in (0, 1) for part in range(PARTS)]
    for kv, n in every:
        source = piece(fresh[kv], n)
        send(("x", kv, n), source, tile(kv, X, n), xpeer)
        send(("other", kv, n), source, tile(kv, OTHER, n), other)

    def open_z():
        @pl.when(odd == 0)
        def _():
            pl.semaphore_wait(zsem, len(across))

        for kv, n in every:
            remote(("zd", kv, n), piece(fresh[kv], n), tile(kv, ZD, n), zdirect).start()

    pl.when(z != 0)(open_z)

    def landed(name, slot):
        for kv, n in every:
            arrived((name, kv, n), tile(kv, slot, n))

    def pass_x(kv, part):
        here = tile(kv, X, part)
        arrived(("x", kv, part), here)
        send(("zf", kv, part), here, tile(kv, ZF, part), zforward)
        send(("xf", kv, part), here, tile(kv, XF, part), other)

    def pass_z(kv, part):
        here = tile(kv, ZF, part)
        arrived(("zf", kv, part), here)
        send(("zff", kv, part), here, tile(kv, ZFF, part), other)

    def pass_on(col, dist, way, kv):
        here = rows(kv, POOLED[(col, dist, way)], 16)
        arrived((col, dist, way, kv), here)
        if dist < 3:
            send((col, dist + 1, way, kv), here, rows(kv, POOLED[(col, dist + 1, way)], 16), ynext[way])
        elif col == "own" and kv == (0 if way == 1 else 1):
            send((col, 4, 1, kv), here, rows(kv, POOLED[(col, 4, 1)], 16), ynext[way])

    def pass_far(kv):
        here = rows(kv, POOLED[("own", 4, 1)], 16)
        arrived(("own", 4, 1, kv), here)
        send(("par", 4, 1, kv), here, rows(kv, POOLED[("par", 4, 1)], 16), partner)

    def ring(col, dist, kvs=(0, 1)):
        for kv in kvs:
            for way in (1, -1):
                pass_on(col, dist, way, kv)

    lane = lax.broadcasted_iota(jnp.int32, (1, 128), 1)

    def penalty(slot):
        col, dist, way = slot
        if slot == ("own", 0, 0):
            return jnp.float32(MASKED * LOG2E)
        half = xh if col == "own" else 1 - xh
        group = half * 8 + (y + 8 - way * dist) % 8
        return age_ref[group].astype(jnp.float32) * jnp.float32(-AGE_PENALTY * LOG2E)

    def bias_of(start, count):
        found = [(o - start, s) for s, o in POOLED.items() if start <= o < start + count]
        if not found:
            return None
        bias = jnp.zeros((1, count), jnp.float32)
        for offset, slot in found:
            here = (lane[:, :count] >= offset) & (lane[:, :count] < offset + 16)
            bias = jnp.where(here, penalty(slot), bias)
        return bias

    scale = LOG2E / (HEAD_DIM ** 0.5)
    heads = q.shape[1] // HEAD_DIM

    def attend(start, count, first=False, last=False):
        bias = bias_of(start, count)

        def block(first_head):
            cols = [
                pl.ds(pl.multiple_of((first_head + u) * HEAD_DIM, HEAD_DIM), HEAD_DIM)
                for u in range(UNROLL)
            ]
            scores = [
                lax.dot_general(
                    q[:, c], kbuf[pl.ds(start, count), c], (((1,), (1,)), ((), ())),
                    preferred_element_type=jnp.float32,
                )
                for c in cols
            ]
            scores = [s * scale if bias is None else s * scale + bias for s in scores]
            peaks = [jnp.max(s, axis=-1, keepdims=True) for s in scores]
            if first:
                tops = [jnp.broadcast_to(peak, (64, HEAD_DIM)) for peak in peaks]
            else:
                olds = [top[:, c] for c in cols]
                tops = [jnp.maximum(old, peak) for old, peak in zip(olds, peaks)]
                keeps = [jnp.exp2(old - new) for old, new in zip(olds, tops)]
            weights = [jnp.exp2(s - new[:, :count]) for s, new in zip(scores, tops)]
            values = [
                jnp.dot(
                    p.astype(jnp.bfloat16), vbuf[pl.ds(start, count), c],
                    preferred_element_type=jnp.float32,
                )
                for p, c in zip(weights, cols)
            ]
            if count < HEAD_DIM:
                rest = jnp.zeros((64, HEAD_DIM - count), jnp.float32)
                weights = [jnp.concatenate([p, rest], axis=1) for p in weights]
            if not first:
                weights = [part[:, c] * keep + p for c, keep, p in zip(cols, keeps, weights)]
                values = [acc[:, c] * keep + v for c, keep, v in zip(cols, keeps, values)]
            if last:
                totals = [jnp.sum(p, axis=-1, keepdims=True) for p in weights]
                for c, total, value in zip(cols, totals, values):
                    out_ref[:, c] = (value / total).astype(jnp.bfloat16)
            else:
                for c, new, p, value in zip(cols, tops, weights, values):
                    top[:, c] = new
                    part[:, c] = p
                    acc[:, c] = value

        @pl.loop(0, heads // UNROLL)
        def _(step):
            block(step * UNROLL)

    ring("own", 1)
    pl.when(z == 0)(open_z)
    sent.extend(
        remote(("zd", kv, n), piece(fresh[kv], n), tile(kv, ZD, n), zdirect) for kv, n in every
    )
    pass_x(0, 0)
    ring("own", 2)
    for kv in (0, 1):
        block = rows(kv, POOLED[("par", 0, 0)], 16)
        arrived(("par0", kv), block)
        for way in (1, -1):
            send(("par", 1, way, kv), block, rows(kv, POOLED[("par", 1, way)], 16), ynext[way])
    for load in loads[2:]:
        load.wait()
    landed("other", OTHER)
    attend(OWN, 128, first=True)
    pass_x(0, 1)
    landed("zd", ZD)
    attend(ZD, 128)
    ring("own", 3)
    pass_x(1, 0)
    ring("par", 1)
    pass_z(0, 0)
    pass_far(0)
    pass_far(1)
    pass_x(1, 1)
    pass_z(0, 1)
    landed("xf", XF)
    attend(X, 128)
    ring("par", 2)
    pass_z(1, 0)
    attend(POOLED[("own", 2, 1)], 128)
    pass_z(1, 1)
    ring("par", 3)
    for kv in (0, 1):
        arrived(("par", 4, 1, kv), rows(kv, POOLED[("par", 4, 1)], 16))
    attend(POOLED[("par", 2, -1)], 64)
    landed("zff", ZFF)
    attend(ZF, 128, last=True)
    for copy in sent:
        copy.wait_send()


def body(queries, keys, values, stale_keys, stale_values, patch_order, stale_age):
    rows, width = queries.shape
    copies = len(IDS)
    wide = (rows, width)
    return pl.pallas_call(
        kernel,
        out_shape=pltpu.VMEM(wide, jnp.bfloat16),
        in_specs=[pl.BlockSpec(memory_space=pl.ANY)] * 5
        + [pl.BlockSpec(memory_space=pltpu.VMEM), pl.BlockSpec(memory_space=pltpu.SMEM)],
        out_specs=pl.BlockSpec(memory_space=pltpu.VMEM),
        scratch_shapes=[
            pltpu.VMEM((ROWS, width), jnp.bfloat16),
            pltpu.VMEM((ROWS, width), jnp.bfloat16),
            pltpu.VMEM(wide, jnp.bfloat16),
            pltpu.VMEM(wide, jnp.bfloat16),
            pltpu.VMEM(wide, jnp.bfloat16),
            pltpu.VMEM(wide, jnp.float32),
            pltpu.VMEM(wide, jnp.float32),
            pltpu.VMEM(wide, jnp.float32),
            pltpu.SemaphoreType.DMA((copies,)),
            pltpu.SemaphoreType.DMA((copies,)),
            pltpu.SemaphoreType.DMA((5,)),
            pltpu.SemaphoreType.REGULAR,
        ],
        name="tile_attention",
        compiler_params=pltpu.CompilerParams(
            collective_id=0, has_side_effects=True, vmem_limit_bytes=56 * 1024 * 1024
        ),
    )(queries, keys, values, stale_keys, stale_values, patch_order.reshape(1, rows), stale_age)


def solution(mesh):
    tokens = P(("group", "blk"), None)
    return jax.shard_map(
        body,
        mesh=mesh,
        in_specs=(tokens, tokens, tokens, tokens, tokens, P(("group", "blk")), P()),
        out_specs=tokens,
        check_vma=False,
    )
```
